256 devices in a mesh: gx: 8 (over z), gy: 32 (over x, y, core).
Axes of the slice: x: 4, y: 4, z: 8, core: 2. Of those that a mesh axis runs over, the one named last changes fastest.
Arguments:
- data: bfloat16 [128, 1024, 4096], P(None, 'gx', 'gy')
- inv_scale: float32 [128], replicated, may hold values from 0.1 to 1
- start: float32 [128, 32], replicated, may hold values from -6 to 6
- rank: int32 [1], replicated, may hold values from 24 to 32
Outputs:
- core: bfloat16 [32, 1024, 4096], P(None, 'gx', 'gy')
- factor: float32 [128, 32], replicated
The draws below stay inside these ranges and needn't reach their ends.
Inputs may be any that keep to these rules, and one draw needn't show every extreme that they name: rank[0] is the number of leading columns of the factor that are kept.
All inputs are finite; a program needn't handle non-finite values.
Results may differ from the reference program's by a relative error of at most 0.0044.
Values sent between devices are 32-bit elements; how exact they have to be, the bound alone decides.
No kernel may reach another device: no remote copies, remote signals or barrier semaphores. Data moves between devices by JAX's collectives and lax.ppermute only.
A program may use at most 64 MiB of HBM per device.

```python
import math
import jax
import jax.numpy as jnp
from jax import lax

V = 128
KMAX = 32
ITERS = 4
CX = 128
NX = 1024
NY = 4096


def draw_data(key, part):
    blocks = NX // CX

    def one_block(index):
        sub_key = jax.random.fold_in(key, index)
        noise = jax.random.normal(sub_key, (V, CX, NY), jnp.float32)
        mixed = noise + 0.5 * jnp.roll(noise, 1, 0) + 0.3 * jnp.roll(noise, 5, 0)
        position = (index * CX + jnp.arange(CX)).astype(jnp.float32) / max(NX - 1, 1)
        ramp = 1.0 + 2.0 * position
        return (mixed * ramp[None, :, None]).astype(jnp.bfloat16)
    stacked = lax.map(one_block, jnp.arange(blocks, dtype=jnp.int32))
    return jnp.transpose(stacked, (1, 0, 2, 3)).reshape(V, NX, NY)


def normal_values(stream_key, dims, deviation, most, held_as=jnp.bfloat16):
    array = deviation * jax.random.normal(stream_key, dims, jnp.float32)
    return jnp.clip(array, min=-most, max=most).astype(held_as)


def setup_inputs(seed: int = 0) -> dict:
    splits = jax.random.split(jax.random.key(seed), 5)
    data = draw_data(jax.random.fold_in(splits[4], 71), 0)
    inv_scale = jnp.clip(jnp.exp(jax.random.uniform(splits[1], (V,), jnp.float32, math.log(0.1), math.log(1.0))), 0.1, 1.0)
    start = normal_values(splits[2], (V, KMAX), 1.0, 6.0, jnp.float32)
    rank = jax.random.randint(splits[3], (1,), KMAX - KMAX // 4, KMAX + 1).astype(jnp.int32)
    return {"data": data, "inv_scale": inv_scale, "start": start, "rank": rank}


def reference(data, inv_scale, start, rank):
    blocks = NX // CX

    def block_gram(index):
        piece = lax.dynamic_slice_in_dim(data, (index * CX).astype(jnp.int32), CX, 1).reshape(V, CX * NY)
        return lax.dot_general(piece.astype(jnp.float32), piece.astype(jnp.float32), (((1,), (1,)), ((), ())), preferred_element_type=jnp.float32)
    gram = jnp.sum(lax.map(block_gram, jnp.arange(blocks, dtype=jnp.int32)), axis=0)
    weighted = inv_scale[:, None] * gram * inv_scale[None, :]
    basis = start
    for turn in range(ITERS):
        image = jnp.dot(weighted, basis, precision=lax.Precision.HIGHEST)
        inner = jnp.dot(image.T, image, precision=lax.Precision.HIGHEST)
        lower = jnp.linalg.cholesky(inner)
        basis = lax.linalg.triangular_solve(lower, image, left_side=False, lower=True, transpose_a=True)
    keep = (jnp.arange(KMAX, dtype=jnp.int32) < rank[0]).astype(jnp.float32)
    factor = basis * keep[None, :]
    scaled_factor = (inv_scale[:, None] * factor).astype(jnp.bfloat16)

    def block_core(index):
        piece = lax.dynamic_slice_in_dim(data, (index * CX).astype(jnp.int32), CX, 1).reshape(V, CX * NY)
        product = lax.dot_general(scaled_factor.astype(jnp.float32), piece.astype(jnp.float32), (((0,), (0,)), ((), ())), preferred_element_type=jnp.float32)
        return product.astype(jnp.bfloat16).reshape(KMAX, CX, NY)
    stacked = lax.map(block_core, jnp.arange(blocks, dtype=jnp.int32))
    core = jnp.transpose(stacked, (1, 0, 2, 3)).reshape(KMAX, NX, NY)
    return (core, factor)
```

```python
import functools

import jax
import jax.numpy as jnp
from jax import lax
from jax.experimental import pallas as pl
from jax.experimental.pallas import tpu as pltpu
from jax.sharding import PartitionSpec as P

ITERS = 4
VMEM = pl.BlockSpec(memory_space=pltpu.VMEM)
SMEM = pl.BlockSpec(memory_space=pltpu.SMEM)
SMALL = pltpu.CompilerParams(vmem_limit_bytes=4 * 2**20)


def split3(x):
    a = x.astype(jnp.bfloat16)
    rest = x - a.astype(jnp.float32)
    b = rest.astype(jnp.bfloat16)
    c = (rest - b.astype(jnp.float32)).astype(jnp.bfloat16)
    return a, b, c


def iota(shape, dim):
    return lax.broadcasted_iota(jnp.int32, shape, dim)


def pack_kernel(gram_ref, out_ref):
    v = gram_ref.shape[0]
    h = v // 2
    gram = gram_ref[...]
    lower_right = pltpu.roll(gram[h:], h, 1)
    row, col = iota((h, v), 0), iota((h, v), 1)
    out_ref[:h] = jnp.where((col >= h) | (row >= col), gram[:h], lower_right)
    diagonal = jnp.sum(jnp.where(iota((v, v), 0) == iota((v, v), 1), gram, 0.0), axis=0, keepdims=True)
    out_ref[h:] = jnp.broadcast_to(diagonal, (out_ref.shape[0] - h, v))


def unpack(packed, v):
    h = v // 2
    q = jnp.concatenate([packed[:h], packed[:h]], axis=0)
    qt = q.T
    row, col = iota((v, v), 0), iota((v, v), 1)
    top = jnp.where((col >= h) | (row >= col), q, qt)
    shifted = pltpu.roll(q, h, 1)
    shifted_t = jnp.concatenate([qt[h:], qt[:h]], axis=0)
    corner = jnp.where(row < col, shifted, shifted_t)
    corner = jnp.where(row == col, packed[h : h + 1], corner)
    bottom = jnp.where(col < h, qt, corner)
    return jnp.where(row < h, top, bottom)


def pair_kernel(a_ref, b_ref, out_ref):
    total = a_ref[...] + b_ref[...]
    for n in range(out_ref.shape[0]):
        out_ref[n] = total


def many_kernel(in_ref, out_ref):
    total = in_ref[0]
    for n in range(1, in_ref.shape[0]):
        total = total + in_ref[n]
    for n in range(out_ref.shape[0]):
        out_ref[n] = total


def eliminate(inner, image, out_ref):
    k_max = inner.shape[0]
    blocks = k_max // 8
    a = [inner[8 * n : 8 * n + 8] for n in range(blocks)]
    y = [image[8 * n : 8 * n + 8] for n in range(blocks)]
    below = iota((8, 1), 0)
    for k in range(k_max):
        b, s = divmod(k, 8)
        row = a[b][s : s + 1]
        r = lax.rsqrt(row[:, k : k + 1])
        ua = row * r
        uy = y[b][s : s + 1] * r
        out_ref[k : k + 1, :] = uy
        for c in range(b, blocks):
            m = a[c][:, k : k + 1] * r
            if c == b:
                m = jnp.where(below > s, m, 0.0)
            a[c] = a[c] - m * ua
            y[c] = y[c] - m * uy


def iterate_kernel(rank_ref, parts_ref, scale_ref, start_ref, factor_ref, scaled_ref, g_ref, basis_ref):
    v = scale_ref.shape[1]
    packed = parts_ref[0]
    for n in range(1, parts_ref.shape[0]):
        packed = packed + parts_ref[n]
    g1, g2, g3 = split3(unpack(packed, v))
    for n, piece in enumerate((g1, g2, g1, g3, g2, g1)):
        g_ref[n * v : (n + 1) * v] = piece
    scale = scale_ref[...]
    basis = start_ref[...]
    for turn in range(ITERS):
        x1, x2, x3 = split3(basis * scale)
        x = jnp.concatenate([x1, x1, x2, x1, x2, x3], axis=1)
        image = jnp.dot(x, g_ref[...], preferred_element_type=jnp.float32) * scale
        y1, y2, y3 = split3(image)
        left = jnp.concatenate([y1, y1, y2, y1, y2, y3], axis=1)
        right = jnp.concatenate([y1, y2, y1, y3, y2, y1], axis=1)
        inner = lax.dot_general(left, right, (((1,), (1,)), ((), ())), preferred_element_type=jnp.float32)
        eliminate(inner, image, basis_ref)
        basis = basis_ref[...]
    factor = jnp.where(iota(basis.shape, 0) < rank_ref[0], basis, 0.0)
    factor_ref[...] = factor
    scaled_ref[...] = (factor * scale).astype(jnp.bfloat16)


def f32(*shape):
    return jax.ShapeDtypeStruct(shape, jnp.float32)


def body(data, inv_scale, start, rank):
    variables, columns = start.shape
    flat = data.reshape(variables, -1)
    gram = lax.dot_general(
        flat, flat, (((1,), (1,)), ((), ())), preferred_element_type=jnp.float32
    )
    rows = variables // 2 + 8
    nx, ny = lax.axis_size("gx"), lax.axis_size("gy")
    packed = pl.pallas_call(
        pack_kernel, out_shape=f32(rows, variables), in_specs=[VMEM], out_specs=VMEM, compiler_params=SMALL
    )(gram)
    other = lax.ppermute(packed, "gy", [(i, i ^ 1) for i in range(ny)])
    cores = [[2 * i + c for i in range(ny // 2)] for c in range(2)]
    sent = pl.pallas_call(
        pair_kernel, out_shape=f32(ny // 2, rows, variables), in_specs=[VMEM] * 2, out_specs=VMEM, compiler_params=SMALL
    )(packed, other)
    got = lax.all_to_all(sent, "gy", 0, 0, axis_index_groups=cores)
    sent = pl.pallas_call(
        many_kernel, out_shape=f32(nx, rows, variables), in_specs=[VMEM], out_specs=VMEM, compiler_params=SMALL
    )(got)
    got = lax.all_to_all(sent, "gx", 0, 0)
    factor_t, scaled_t = pl.pallas_call(
        iterate_kernel,
        out_shape=(f32(columns, variables), jax.ShapeDtypeStruct((columns, variables), jnp.bfloat16)),
        in_specs=[SMEM, VMEM, VMEM, VMEM],
        out_specs=(VMEM, VMEM),
        compiler_params=SMALL,
        scratch_shapes=[
            pltpu.VMEM((6 * variables, variables), jnp.bfloat16),
            pltpu.VMEM((columns, variables), jnp.float32),
        ],
    )(rank, got, inv_scale[None, :], start.T)
    product = lax.dot_general(
        scaled_t, flat, (((1,), (0,)), ((), ())), preferred_element_type=jnp.float32
    )
    core = product.astype(jnp.bfloat16).reshape(columns, data.shape[1], data.shape[2])
    return (core, factor_t.T)


def solution(mesh):
    in_specs = (P(None, "gx", "gy"), P(), P(), P())
    out_specs = (P(None, "gx", "gy"), P())
    return jax.shard_map(body, mesh=mesh, in_specs=in_specs, out_specs=out_specs, check_vma=False)
```

```python
import functools

import jax
import jax.numpy as jnp
from jax import lax
from jax.experimental import pallas as pl
from jax.experimental.pallas import tpu as pltpu
from jax.sharding import PartitionSpec as P

ITERS = 4
ROWS = 16
VMEM = pl.BlockSpec(memory_space=pltpu.VMEM)
SMEM = pl.BlockSpec(memory_space=pltpu.SMEM)
ANY = pl.BlockSpec(memory_space=pl.ANY)
SMALL = pltpu.CompilerParams(vmem_limit_bytes=4 * 2**20)
MOST = pltpu.CompilerParams(vmem_limit_bytes=50 * 2**20)
LARGE = pltpu.CompilerParams(vmem_limit_bytes=16 * 2**20)


def iota(shape, dim):
    return lax.broadcasted_iota(jnp.int32, shape, dim)


def f32(*shape):
    return jax.ShapeDtypeStruct(shape, jnp.float32)


def split3(x):
    a = x.astype(jnp.bfloat16)
    rest = x - a.astype(jnp.float32)
    b = rest.astype(jnp.bfloat16)
    c = (rest - b.astype(jnp.float32)).astype(jnp.bfloat16)
    return a, b, c


def fetch(data_ref, held_ref, sem):
    return [
        pltpu.make_async_copy(
            data_ref.at[:, pl.ds(ROWS * n, ROWS), :], held_ref.at[n], sem.at[n]
        )
        for n in range(held_ref.shape[0])
    ]


def columns_of(block):
    t = jnp.swapaxes(block, 0, 1)
    return jnp.concatenate([t[i] for i in range(t.shape[0])], axis=1)


def gram_kernel(data_ref, mine_ref, theirs_ref, held_ref, sem, *, axis):
    copies = fetch(data_ref, held_ref, sem)
    for copy in copies:
        copy.start()
    v = held_ref.shape[1]
    h = v // 2
    gram = jnp.zeros((v, v), jnp.float32)
    for n, copy in enumerate(copies):
        copy.wait()
        x = columns_of(held_ref[n])
        gram = gram + lax.dot_general(x, x, (((1,), (1,)), ((), ())), preferred_element_type=jnp.float32)
    lower_right = pltpu.roll(gram[h:], h, 1)
    row, col = iota((h, v), 0), iota((h, v), 1)
    top = jnp.where((col >= h) | (row >= col), gram[:h], lower_right)
    diagonal = jnp.sum(jnp.where(iota((v, v), 0) == iota((v, v), 1), gram, 0.0), axis=0, keepdims=True)
    lower = lax.rem(lax.axis_index(axis), 2) == 0
    first, second = top[: h // 2], top[h // 2 :]
    mine_ref[: h // 2] = jnp.where(lower, first, second)
    theirs_ref[: h // 2] = jnp.where(lower, second, first)
    diagonal = jnp.broadcast_to(diagonal, (mine_ref.shape[0] - h // 2, v))
    mine_ref[h // 2 :] = diagonal
    theirs_ref[h // 2 :] = diagonal


def unpack(first, second, v):
    h = v // 2
    q = jnp.concatenate([first[: h // 2], second[: h // 2]] * 2, axis=0)
    qt = q.T
    row, col = iota((v, v), 0), iota((v, v), 1)
    top = jnp.where((col >= h) | (row >= col), q, qt)
    shifted = pltpu.roll(q, h, 1)
    shifted_t = jnp.concatenate([qt[h:], qt[:h]], axis=0)
    corner = jnp.where(row < col, shifted, shifted_t)
    corner = jnp.where(row == col, first[h // 2 : h // 2 + 1], corner)
    bottom = jnp.where(col < h, qt, corner)
    return jnp.where(row < h, top, bottom)


def pair_kernel(mine_ref, theirs_ref, out_ref):
    total = mine_ref[...] + theirs_ref[...]
    for n in range(out_ref.shape[0]):
        out_ref[n] = total


def total_of(ref):
    total = ref[0]
    for n in range(1, ref.shape[0]):
        total = total + ref[n]
    return total


def many_kernel(in_ref, out_ref):
    total = total_of(in_ref)
    for n in range(out_ref.shape[0]):
        out_ref[n] = total


def sum_kernel(in_ref, out_ref):
    out_ref[...] = total_of(in_ref)


def eliminate(inner, image, out_ref, beside):
    n, v = image.shape
    blocks = n // 8
    a = [inner[8 * c : 8 * c + 8] for c in range(blocks)]
    y = [image[8 * c : 8 * c + 8] for c in range(blocks)]

    def full(x):
        return jnp.broadcast_to(x, (8, v))

    for b in range(blocks):
        beside(b)
        rows_a = [jnp.broadcast_to(a[b][t : t + 1], (8, n)) for t in range(8)]
        rows_y = [full(y[b][t : t + 1]) for t in range(8)]
        cols = {c: [full(a[c][:, 8 * b + t : 8 * b + t + 1]) for t in range(8)] for c in range(b + 1, blocks)}
        p = [[full(a[b][t : t + 1, 8 * b + u : 8 * b + u + 1]) for u in range(t + 1)] for t in range(8)]
        for u in range(8):
            r = lax.rsqrt(p[u][u])
            low = {t: p[t][u] * r for t in range(u + 1, 8)}
            for t in low:
                for x in range(u + 1, t + 1):
                    p[t][x] = p[t][x] - low[t] * low[x]
            rows_a[u] = rows_a[u] * r[:, :n]
            rows_y[u] = rows_y[u] * r
            for c in cols:
                cols[c][u] = cols[c][u] * r
            for t in low:
                rows_a[t] = rows_a[t] - low[t][:, :n] * rows_a[u]
                rows_y[t] = rows_y[t] - low[t] * rows_y[u]
                for c in cols:
                    cols[c][t] = cols[c][t] - low[t] * cols[c][u]
            out_ref[8 * b + u : 8 * b + u + 1, :] = rows_y[u][:1]
        for c in cols:
            for u in range(8):
                a[c] = a[c] - cols[c][u][:, :n] * rows_a[u]
                y[c] = y[c] - cols[c][u] * rows_y[u]


def final_kernel(
    rank_ref, mine_ref, theirs_ref, scale_ref, start_ref, data_ref, factor_ref, core_ref,
    turned_ref, held_ref, g_ref, basis_ref, sem, *, axis
):
    v = scale_ref.shape[1]
    pieces = held_ref.shape[0]
    blocks = start_ref.shape[0] // 8

    def turn_data(turn, b):
        shares = ITERS * blocks
        first, last = ((turn * blocks + b + end) * pieces * 2 // shares for end in (0, 1))
        for n in range(first, last):
            piece, half = divmod(n, 2)
            some = slice(half * (v // 2), (half + 1) * (v // 2))
            rows = slice(piece * ROWS, (piece + 1) * ROWS)
            turned_ref[piece, :, some, :] = jnp.swapaxes(data_ref[some, rows, :], 0, 1)

    lower = lax.rem(lax.axis_index(axis), 2) == 0
    mine, theirs = mine_ref[...], theirs_ref[...]
    g1, g2, g3 = split3(unpack(jnp.where(lower, mine, theirs), jnp.where(lower, theirs, mine), v))
    for n, piece in enumerate((g1, g2, g1, g3, g2, g1)):
        g_ref[n * v : (n + 1) * v] = piece
    scale = scale_ref[...]
    basis = start_ref[...]
    for turn in range(ITERS):
        x1, x2, x3 = split3(basis * scale)
        x = jnp.concatenate([x1, x1, x2, x1, x2, x3], axis=1)
        image = jnp.dot(x, g_ref[...], preferred_element_type=jnp.float32) * scale
        y1, y2, y3 = split3(image)
        left = jnp.concatenate([y1, y1, y2, y1, y2, y3], axis=1)
        right = jnp.concatenate([y1, y2, y1, y3, y2, y1], axis=1)
        inner = lax.dot_general(left, right, (((1,), (1,)), ((), ())), preferred_element_type=jnp.float32)
        eliminate(inner, image, basis_ref, functools.partial(turn_data, turn))
        basis = basis_ref[...]
    factor = jnp.where(iota(basis.shape, 0) < rank_ref[0], basis, 0.0)
    factor_ref[...] = factor
    scaled = (factor * scale).astype(jnp.bfloat16)
    outs = []
    for n in range(pieces):
        product = [
            jnp.dot(scaled, turned_ref[n, i], preferred_element_type=jnp.float32).astype(jnp.bfloat16)
            for i in range(ROWS)
        ]
        held_ref[n] = jnp.swapaxes(jnp.stack(product), 0, 1)
        outs.append(
            pltpu.make_async_copy(held_ref.at[n], core_ref.at[:, pl.ds(ROWS * n, ROWS), :], sem.at[n])
        )
        outs[-1].start()
    for copy in outs:
        copy.wait()


def gram_call(data, axis="gy"):
    variables, rows, cells = data.shape
    pieces = rows // ROWS
    return pl.pallas_call(
        functools.partial(gram_kernel, axis=axis),
        out_shape=(f32(variables // 4 + 8, variables),) * 2,
        in_specs=[ANY],
        out_specs=(VMEM, VMEM),
        compiler_params=MOST,
        scratch_shapes=[
            pltpu.VMEM((pieces, variables, ROWS, cells), jnp.bfloat16),
            pltpu.SemaphoreType.DMA((pieces,)),
        ],
    )(data)


def final_call(rank, mine, theirs, inv_scale, start, data, axis="gy"):
    variables, rows, cells = data.shape
    columns = start.shape[1]
    pieces = rows // ROWS
    return pl.pallas_call(
        functools.partial(final_kernel, axis=axis),
        out_shape=(f32(columns, variables), jax.ShapeDtypeStruct((columns, rows, cells), jnp.bfloat16)),
        in_specs=[SMEM, VMEM, VMEM, VMEM, VMEM, VMEM],
        out_specs=(VMEM, ANY),
        compiler_params=LARGE,
        scratch_shapes=[
            pltpu.VMEM((pieces, ROWS, variables, cells), jnp.bfloat16),
            pltpu.VMEM((pieces, columns, ROWS, cells), jnp.bfloat16),
            pltpu.VMEM((6 * variables, variables), jnp.bfloat16),
            pltpu.VMEM((columns, variables), jnp.float32),
            pltpu.SemaphoreType.DMA((pieces,)),
        ],
    )(rank, mine, theirs, inv_scale[None, :], start.T, data)


def call(kernel, shape, *args):
    return pl.pallas_call(
        kernel, out_shape=f32(*shape), in_specs=[VMEM] * len(args), out_specs=VMEM, compiler_params=SMALL
    )(*args)


def body(data, inv_scale, start, rank):
    variables = data.shape[0]
    nx, ny = lax.axis_size("gx"), lax.axis_size("gy")
    swap = [(i, i ^ 1) for i in range(ny)]
    cores = [[2 * i + c for i in range(ny // 2)] for c in range(2)]
    mine, theirs = gram_call(data)
    theirs = lax.ppermute(theirs, "gy", swap)
    piece = mine.shape
    got = lax.all_to_all(
        call(pair_kernel, (ny // 2, *piece), mine, theirs), "gy", 0, 0, axis_index_groups=cores
    )
    got = lax.all_to_all(call(many_kernel, (nx, *piece), got), "gx", 0, 0)
    mine = call(sum_kernel, piece, got)
    theirs = lax.ppermute(mine, "gy", swap)
    factor_t, core = final_call(rank, mine, theirs, inv_scale, start, data)
    return (core, factor_t.T)


def solution(mesh):
    in_specs = (P(None, "gx", "gy"), P(), P(), P())
    out_specs = (P(None, "gx", "gy"), P())
    return jax.shard_map(body, mesh=mesh, in_specs=in_specs, out_specs=out_specs, check_vma=False)
```

```python
import functools

import jax
import jax.numpy as jnp
from jax import lax
from jax.experimental import pallas as pl
from jax.experimental.pallas import tpu as pltpu
from jax.sharding import PartitionSpec as P

ITERS = 4
ROWS = 16
VMEM = pl.BlockSpec(memory_space=pltpu.VMEM)
SMEM = pl.BlockSpec(memory_space=pltpu.SMEM)
ANY = pl.BlockSpec(memory_space=pl.ANY)
SMALL = pltpu.CompilerParams(vmem_limit_bytes=4 * 2**20)
MOST = pltpu.CompilerParams(vmem_limit_bytes=50 * 2**20)
LARGE = pltpu.CompilerParams(vmem_limit_bytes=16 * 2**20)


def iota(shape, dim):
    return lax.broadcasted_iota(jnp.int32, shape, dim)


def f32(*shape):
    return jax.ShapeDtypeStruct(shape, jnp.float32)


def split3(x):
    a = x.astype(jnp.bfloat16)
    rest = x - a.astype(jnp.float32)
    b = rest.astype(jnp.bfloat16)
    c = (rest - b.astype(jnp.float32)).astype(jnp.bfloat16)
    return a, b, c


def fetch(data_ref, held_ref, sem):
    return [
        pltpu.make_async_copy(
            data_ref.at[:, pl.ds(ROWS * n, ROWS), :], held_ref.at[n], sem.at[n]
        )
        for n in range(held_ref.shape[0])
    ]


def columns_of(block):
    t = jnp.swapaxes(block, 0, 1)
    return jnp.concatenate([t[i] for i in range(t.shape[0])], axis=1)


def gram_kernel(data_ref, mine_ref, theirs_ref, held_ref, sem, *, axis):
    copies = fetch(data_ref, held_ref, sem)
    for copy in copies:
        copy.start()
    v = held_ref.shape[1]
    h = v // 2
    gram = jnp.zeros((v, v), jnp.float32)
    for n, copy in enumerate(copies):
        copy.wait()
        x = columns_of(held_ref[n])
        gram = gram + lax.dot_general(x, x, (((1,), (1,)), ((), ())), preferred_element_type=jnp.float32)
    lower_right = pltpu.roll(gram[h:], h, 1)
    row, col = iota((h, v), 0), iota((h, v), 1)
    top = jnp.where((col >= h) | (row >= col), gram[:h], lower_right)
    diagonal = jnp.sum(jnp.where(iota((v, v), 0) == iota((v, v), 1), gram, 0.0), axis=0, keepdims=True)
    lower = lax.rem(lax.axis_index(axis), 2) == 0
    first, second = top[: h // 2], top[h // 2 :]
    mine_ref[: h // 2] = jnp.where(lower, first, second)
    theirs_ref[: h // 2] = jnp.where(lower, second, first)
    diagonal = jnp.broadcast_to(diagonal, (mine_ref.shape[0] - h // 2, v))
    mine_ref[h // 2 :] = diagonal
    theirs_ref[h // 2 :] = diagonal


def unpack(first, second, v):
    h = v // 2
    q = jnp.concatenate([first[: h // 2], second[: h // 2]] * 2, axis=0)
    qt = q.T
    row, col = iota((v, v), 0), iota((v, v), 1)
    top = jnp.where((col >= h) | (row >= col), q, qt)
    shifted = pltpu.roll(q, h, 1)
    shifted_t = jnp.concatenate([qt[h:], qt[:h]], axis=0)
    corner = jnp.where(row < col, shifted, shifted_t)
    corner = jnp.where(row == col, first[h // 2 : h // 2 + 1], corner)
    bottom = jnp.where(col < h, qt, corner)
    return jnp.where(row < h, top, bottom)


def pair_kernel(mine_ref, theirs_ref, out_ref):
    count, lines, v = out_ref.shape[1:]
    total = (mine_ref[...] + theirs_ref[...])[: count * lines].reshape(count, lines, v)
    for n in range(out_ref.shape[0]):
        out_ref[n] = total


def total_of(ref):
    total = ref[0]
    for n in range(1, ref.shape[0]):
        total = total + ref[n]
    return total


def many_kernel(in_ref, out_ref):
    total = total_of(in_ref)
    for n in range(out_ref.shape[0]):
        out_ref[n] = total


def sum_kernel(in_ref, out_ref):
    total = total_of(in_ref)
    rows = total.shape[0] * total.shape[1]
    out_ref[:rows] = total.reshape(rows, total.shape[2])
    out_ref[rows:] = jnp.zeros((out_ref.shape[0] - rows, out_ref.shape[1]), jnp.float32)


def eliminate(inner, image, out_ref, beside):
    n, v = image.shape
    blocks = n // 8
    a = [inner[8 * c : 8 * c + 8] for c in range(blocks)]
    y = [image[8 * c : 8 * c + 8] for c in range(blocks)]

    def full(x):
        return jnp.broadcast_to(x, (8, v))

    for b in range(blocks):
        beside(b)
        rows_a = [jnp.broadcast_to(a[b][t : t + 1], (8, n)) for t in range(8)]
        rows_y = [full(y[b][t : t + 1]) for t in range(8)]
        cols = {c: [full(a[c][:, 8 * b + t : 8 * b + t + 1]) for t in range(8)] for c in range(b + 1, blocks)}
        pivot = [full(a[b][:, 8 * b + u : 8 * b + u + 1]) for u in range(8)]
        p = [[full(pivot[u][t : t + 1]) for u in range(t + 1)] for t in range(8)]
        for u in range(8):
            r = lax.rsqrt(p[u][u])
            low = {t: p[t][u] * r for t in range(u + 1, 8)}
            for t in low:
                for x in range(u + 1, t + 1):
                    p[t][x] = p[t][x] - low[t] * low[x]
            rows_a[u] = rows_a[u] * r[:, :n]
            rows_y[u] = rows_y[u] * r
            for c in cols:
                cols[c][u] = cols[c][u] * r
            for t in low:
                rows_a[t] = rows_a[t] - low[t][:, :n] * rows_a[u]
                rows_y[t] = rows_y[t] - low[t] * rows_y[u]
                for c in cols:
                    cols[c][t] = cols[c][t] - low[t] * cols[c][u]
            out_ref[8 * b + u : 8 * b + u + 1, :] = rows_y[u][:1]
        for c in cols:
            for u in range(8):
                a[c] = a[c] - cols[c][u][:, :n] * rows_a[u]
                y[c] = y[c] - cols[c][u] * rows_y[u]


def final_kernel(
    rank_ref, mine_ref, theirs_ref, scale_ref, start_ref, data_ref, factor_ref, core_ref,
    turned_ref, held_ref, g_ref, basis_ref, sem, *, axis
):
    v = scale_ref.shape[1]
    pieces = held_ref.shape[0]
    blocks = start_ref.shape[0] // 8

    def turn_data(turn, b):
        shares = ITERS * blocks
        first, last = ((turn * blocks + b + end) * pieces * 2 // shares for end in (0, 1))
        for n in range(first, last):
            piece, half = divmod(n, 2)
            some = slice(half * (v // 2), (half + 1) * (v // 2))
            rows = slice(piece * ROWS, (piece + 1) * ROWS)
            turned_ref[piece, :, some, :] = jnp.swapaxes(data_ref[some, rows, :], 0, 1)

    lower = lax.rem(lax.axis_index(axis), 2) == 0
    mine, theirs = mine_ref[...], theirs_ref[...]
    g1, g2, g3 = split3(unpack(jnp.where(lower, mine, theirs), jnp.where(lower, theirs, mine), v))
    for n, piece in enumerate((g1, g2, g1, g3, g2, g1)):
        g_ref[n * v : (n + 1) * v] = piece
    scale = scale_ref[...]

    def weigh(x):
        x1, x2, x3 = split3(x * scale)
        x = jnp.concatenate([x1, x1, x2, x1, x2, x3], axis=1)
        return jnp.dot(x, g_ref[...], preferred_element_type=jnp.float32) * scale

    image = weigh(start_ref[...])
    for turn in range(ITERS):
        y1, y2, y3 = split3(image)
        left = jnp.concatenate([y1, y1, y2, y1, y2, y3], axis=1)
        right = jnp.concatenate([y1, y2, y1, y3, y2, y1], axis=1)
        inner = lax.dot_general(left, right, (((1,), (1,)), ((), ())), preferred_element_type=jnp.float32)
        solved = weigh(image) if turn < ITERS - 1 else image
        eliminate(inner, solved, basis_ref, functools.partial(turn_data, turn))
        image = basis_ref[...]
    basis = image
    factor = jnp.where(iota(basis.shape, 0) < rank_ref[0], basis, 0.0)
    factor_ref[...] = factor
    scaled = (factor * scale).astype(jnp.bfloat16)
    outs = []
    for n in range(pieces):
        product = [
            jnp.dot(scaled, turned_ref[n, i], preferred_element_type=jnp.float32).astype(jnp.bfloat16)
            for i in range(ROWS)
        ]
        held_ref[n] = jnp.swapaxes(jnp.stack(product), 0, 1)
        outs.append(
            pltpu.make_async_copy(held_ref.at[n], core_ref.at[:, pl.ds(ROWS * n, ROWS), :], sem.at[n])
        )
        outs[-1].start()
    for copy in outs:
        copy.wait()


def gram_call(data, axis="gy"):
    variables, rows, cells = data.shape
    pieces = rows // ROWS
    return pl.pallas_call(
        functools.partial(gram_kernel, axis=axis),
        out_shape=(f32(variables // 4 + 8, variables),) * 2,
        in_specs=[ANY],
        out_specs=(VMEM, VMEM),
        compiler_params=MOST,
        scratch_shapes=[
            pltpu.VMEM((pieces, variables, ROWS, cells), jnp.bfloat16),
            pltpu.SemaphoreType.DMA((pieces,)),
        ],
    )(data)


def final_call(rank, mine, theirs, inv_scale, start, data, axis="gy"):
    variables, rows, cells = data.shape
    columns = start.shape[1]
    pieces = rows // ROWS
    return pl.pallas_call(
        functools.partial(final_kernel, axis=axis),
        out_shape=(f32(columns, variables), jax.ShapeDtypeStruct((columns, rows, cells), jnp.bfloat16)),
        in_specs=[SMEM, VMEM, VMEM, VMEM, VMEM, VMEM],
        out_specs=(VMEM, ANY),
        compiler_params=LARGE,
        scratch_shapes=[
            pltpu.VMEM((pieces, ROWS, variables, cells), jnp.bfloat16),
            pltpu.VMEM((pieces, columns, ROWS, cells), jnp.bfloat16),
            pltpu.VMEM((6 * variables, variables), jnp.bfloat16),
            pltpu.VMEM((columns, variables), jnp.float32),
            pltpu.SemaphoreType.DMA((pieces,)),
        ],
    )(rank, mine, theirs, inv_scale[None, :], start.T, data)


def call(kernel, shape, *args):
    return pl.pallas_call(
        kernel, out_shape=f32(*shape), in_specs=[VMEM] * len(args), out_specs=VMEM, compiler_params=SMALL
    )(*args)


def body(data, inv_scale, start, rank):
    variables = data.shape[0]
    nx, ny = lax.axis_size("gx"), lax.axis_size("gy")
    swap = [(i, i ^ 1) for i in range(ny)]
    cores = [[2 * i + c for i in range(ny // 2)] for c in range(2)]
    mine, theirs = gram_call(data)
    theirs = lax.ppermute(theirs, "gy", swap)
    piece = (variables // 16 + 1, 4, variables)
    got = lax.all_to_all(
        call(pair_kernel, (ny // 2, *piece), mine, theirs), "gy", 0, 0, axis_index_groups=cores
    )
    got = lax.all_to_all(call(many_kernel, (nx, *piece), got), "gx", 0, 0)
    mine = call(sum_kernel, theirs.shape, got)
    theirs = lax.ppermute(mine, "gy", swap)
    factor_t, core = final_call(rank, mine, theirs, inv_scale, start, data)
    return (core, factor_t.T)


def solution(mesh):
    in_specs = (P(None, "gx", "gy"), P(), P(), P())
    out_specs = (P(None, "gx", "gy"), P())
    return jax.shard_map(body, mesh=mesh, in_specs=in_specs, out_specs=out_specs, check_vma=False)
```

```python
import functools

import jax
import jax.numpy as jnp
from jax import lax
from jax.experimental import pallas as pl
from jax.experimental.pallas import tpu as pltpu
from jax.sharding import PartitionSpec as P

ITERS = 4
ROWS = 16
VMEM = pl.BlockSpec(memory_space=pltpu.VMEM)
SMEM = pl.BlockSpec(memory_space=pltpu.SMEM)
ANY = pl.BlockSpec(memory_space=pl.ANY)
SMALL = pltpu.CompilerParams(vmem_limit_bytes=4 * 2**20)
MOST = pltpu.CompilerParams(vmem_limit_bytes=50 * 2**20)
LARGE = pltpu.CompilerParams(vmem_limit_bytes=16 * 2**20)


def iota(shape, dim):
    return lax.broadcasted_iota(jnp.int32, shape, dim)


def f32(*shape):
    return jax.ShapeDtypeStruct(shape, jnp.float32)


def split3(x):
    a = x.astype(jnp.bfloat16)
    rest = x - a.astype(jnp.float32)
    b = rest.astype(jnp.bfloat16)
    c = (rest - b.astype(jnp.float32)).astype(jnp.bfloat16)
    return a, b, c


def fetch(data_ref, held_ref, sem):
    return [
        pltpu.make_async_copy(
            data_ref.at[:, pl.ds(ROWS * n, ROWS), :], held_ref.at[n], sem.at[n]
        )
        for n in range(held_ref.shape[0])
    ]


def columns_of(block):
    t = jnp.swapaxes(block, 0, 1)
    return jnp.concatenate([t[i] for i in range(t.shape[0])], axis=1)


def gram_kernel(data_ref, mine_ref, theirs_ref, held_ref, sem, *, axis):
    copies = fetch(data_ref, held_ref, sem)
    for copy in copies:
        copy.start()
    v = held_ref.shape[1]
    h = v // 2
    gram = jnp.zeros((v, v), jnp.float32)
    for n, copy in enumerate(copies):
        copy.wait()
        x = columns_of(held_ref[n])
        gram = gram + lax.dot_general(x, x, (((1,), (1,)), ((), ())), preferred_element_type=jnp.float32)
    lower_right = pltpu.roll(gram[h:], h, 1)
    row, col = iota((h, v), 0), iota((h, v), 1)
    top = jnp.where((col >= h) | (row >= col), gram[:h], lower_right)
    diagonal = jnp.sum(jnp.where(iota((v, v), 0) == iota((v, v), 1), gram, 0.0), axis=0, keepdims=True)
    lower = lax.rem(lax.axis_index(axis), 2) == 0
    first, second = top[: h // 2], top[h // 2 :]
    mine_ref[: h // 2] = jnp.where(lower, first, second)
    theirs_ref[: h // 2] = jnp.where(lower, second, first)
    diagonal = jnp.broadcast_to(diagonal, (mine_ref.shape[0] - h // 2, v))
    mine_ref[h // 2 :] = diagonal
    theirs_ref[h // 2 :] = diagonal


def unpack(first, second, v):
    h = v // 2
    q = jnp.concatenate([first[: h // 2], second[: h // 2]] * 2, axis=0)
    qt = q.T
    row, col = iota((v, v), 0), iota((v, v), 1)
    top = jnp.where((col >= h) | (row >= col), q, qt)
    shifted = pltpu.roll(q, h, 1)
    shifted_t = jnp.concatenate([qt[h:], qt[:h]], axis=0)
    corner = jnp.where(row < col, shifted, shifted_t)
    corner = jnp.where(row == col, first[h // 2 : h // 2 + 1], corner)
    bottom = jnp.where(col < h, qt, corner)
    return jnp.where(row < h, top, bottom)


def pair_kernel(mine_ref, theirs_ref, out_ref):
    count, lines, v = out_ref.shape[1:]
    total = (mine_ref[...] + theirs_ref[...])[: count * lines].reshape(count, lines, v)
    for n in range(out_ref.shape[0]):
        out_ref[n] = total


def total_of(ref):
    total = ref[0]
    for n in range(1, ref.shape[0]):
        total = total + ref[n]
    return total


def add_kernel(*refs):
    total = refs[0][...]
    for ref in refs[1:-1]:
        total = total + ref[...]
    refs[-1][...] = total


def sum_kernel(in_ref, out_ref):
    total = total_of(in_ref)
    rows = total.shape[0] * total.shape[1]
    out_ref[:rows] = total.reshape(rows, total.shape[2])
    out_ref[rows:] = jnp.zeros((out_ref.shape[0] - rows, out_ref.shape[1]), jnp.float32)


def eliminate(inner, image, out_ref, beside):
    n, v = image.shape
    blocks = n // 8
    a = [inner[8 * c : 8 * c + 8] for c in range(blocks)]
    y = [image[8 * c : 8 * c + 8] for c in range(blocks)]

    def full(x):
        return jnp.broadcast_to(x, (8, v))

    for b in range(blocks):
        beside(b)
        rows_a = [jnp.broadcast_to(a[b][t : t + 1], (8, n)) for t in range(8)]
        rows_y = [full(y[b][t : t + 1]) for t in range(8)]
        cols = {c: [full(a[c][:, 8 * b + t : 8 * b + t + 1]) for t in range(8)] for c in range(b + 1, blocks)}
        pivot = [full(a[b][:, 8 * b + u : 8 * b + u + 1]) for u in range(8)]
        p = [[full(pivot[u][t : t + 1]) for u in range(t + 1)] for t in range(8)]
        for u in range(8):
            r = lax.rsqrt(p[u][u])
            low = {t: p[t][u] * r for t in range(u + 1, 8)}
            for t in low:
                for x in range(u + 1, t + 1):
                    p[t][x] = p[t][x] - low[t] * low[x]
            rows_a[u] = rows_a[u] * r[:, :n]
            rows_y[u] = rows_y[u] * r
            for c in cols:
                cols[c][u] = cols[c][u] * r
            for t in low:
                rows_a[t] = rows_a[t] - low[t][:, :n] * rows_a[u]
                rows_y[t] = rows_y[t] - low[t] * rows_y[u]
                for c in cols:
                    cols[c][t] = cols[c][t] - low[t] * cols[c][u]
            out_ref[8 * b + u : 8 * b + u + 1, :] = rows_y[u][:1]
        for c in cols:
            for u in range(8):
                a[c] = a[c] - cols[c][u][:, :n] * rows_a[u]
                y[c] = y[c] - cols[c][u] * rows_y[u]


def final_kernel(
    rank_ref, mine_ref, theirs_ref, scale_ref, start_ref, data_ref, factor_ref, core_ref,
    turned_ref, held_ref, g_ref, basis_ref, sem, *, axis
):
    v = scale_ref.shape[1]
    pieces = held_ref.shape[0]
    blocks = start_ref.shape[0] // 8

    def turn_data(turn, b):
        shares = ITERS * blocks
        first, last = ((turn * blocks + b + end) * pieces * 2 // shares for end in (0, 1))
        for n in range(first, last):
            piece, half = divmod(n, 2)
            some = slice(half * (v // 2), (half + 1) * (v // 2))
            rows = slice(piece * ROWS, (piece + 1) * ROWS)
            turned_ref[piece, :, some, :] = jnp.swapaxes(data_ref[some, rows, :], 0, 1)

    lower = lax.rem(lax.axis_index(axis), 2) == 0
    mine, theirs = mine_ref[...], theirs_ref[...]
    g1, g2, g3 = split3(unpack(jnp.where(lower, mine, theirs), jnp.where(lower, theirs, mine), v))
    for n, piece in enumerate((g1, g2, g1, g3, g2, g1)):
        g_ref[n * v : (n + 1) * v] = piece
    scale = scale_ref[...]

    def weigh(x):
        x1, x2, x3 = split3(x * scale)
        x = jnp.concatenate([x1, x1, x2, x1, x2, x3], axis=1)
        return jnp.dot(x, g_ref[...], preferred_element_type=jnp.float32) * scale

    image = weigh(start_ref[...])
    for turn in range(ITERS):
        y1, y2, y3 = split3(image)
        left = jnp.concatenate([y1, y1, y2, y1, y2, y3], axis=1)
        right = jnp.concatenate([y1, y2, y1, y3, y2, y1], axis=1)
        inner = lax.dot_general(left, right, (((1,), (1,)), ((), ())), preferred_element_type=jnp.float32)
        solved = weigh(image) if turn < ITERS - 1 else image
        eliminate(inner, solved, basis_ref, functools.partial(turn_data, turn))
        image = basis_ref[...]
    basis = image
    factor = jnp.where(iota(basis.shape, 0) < rank_ref[0], basis, 0.0)
    factor_ref[...] = factor
    scaled = (factor * scale).astype(jnp.bfloat16)
    outs = []
    for n in range(pieces):
        product = [
            jnp.dot(scaled, turned_ref[n, i], preferred_element_type=jnp.float32).astype(jnp.bfloat16)
            for i in range(ROWS)
        ]
        held_ref[n] = jnp.swapaxes(jnp.stack(product), 0, 1)
        outs.append(
            pltpu.make_async_copy(held_ref.at[n], core_ref.at[:, pl.ds(ROWS * n, ROWS), :], sem.at[n])
        )
        outs[-1].start()
    for copy in outs:
        copy.wait()


def gram_call(data, axis="gy"):
    variables, rows, cells = data.shape
    pieces = rows // ROWS
    return pl.pallas_call(
        functools.partial(gram_kernel, axis=axis),
        out_shape=(f32(variables // 4 + 8, variables),) * 2,
        in_specs=[ANY],
        out_specs=(VMEM, VMEM),
        compiler_params=MOST,
        scratch_shapes=[
            pltpu.VMEM((pieces, variables, ROWS, cells), jnp.bfloat16),
            pltpu.SemaphoreType.DMA((pieces,)),
        ],
    )(data)


def final_call(rank, mine, theirs, inv_scale, start, data, axis="gy"):
    variables, rows, cells = data.shape
    columns = start.shape[1]
    pieces = rows // ROWS
    return pl.pallas_call(
        functools.partial(final_kernel, axis=axis),
        out_shape=(f32(columns, variables), jax.ShapeDtypeStruct((columns, rows, cells), jnp.bfloat16)),
        in_specs=[SMEM, VMEM, VMEM, VMEM, VMEM, VMEM],
        out_specs=(VMEM, ANY),
        compiler_params=LARGE,
        scratch_shapes=[
            pltpu.VMEM((pieces, ROWS, variables, cells), jnp.bfloat16),
            pltpu.VMEM((pieces, columns, ROWS, cells), jnp.bfloat16),
            pltpu.VMEM((6 * variables, variables), jnp.bfloat16),
            pltpu.VMEM((columns, variables), jnp.float32),
            pltpu.SemaphoreType.DMA((pieces,)),
        ],
    )(rank, mine, theirs, inv_scale[None, :], start.T, data)


def call(kernel, shape, *args):
    return pl.pallas_call(
        kernel, out_shape=f32(*shape), in_specs=[VMEM] * len(args), out_specs=VMEM, compiler_params=SMALL
    )(*args)


def body(data, inv_scale, start, rank):
    variables = data.shape[0]
    nx, ny = lax.axis_size("gx"), lax.axis_size("gy")
    swap = [(i, i ^ 1) for i in range(ny)]
    cores = [[2 * i + c for i in range(ny // 2)] for c in range(2)]
    mine, theirs = gram_call(data)
    theirs = lax.ppermute(theirs, "gy", swap)
    piece = (variables // 16 + 1, 4, variables)
    mine = call(add_kernel, mine.shape, mine, theirs)
    theirs = [lax.ppermute(mine, "gx", [(n, n ^ d) for n in range(nx)]) for d in (1, 2, 3)]
    mine = call(add_kernel, mine.shape, mine, *theirs)
    theirs = lax.ppermute(mine, "gx", [(n, n ^ (nx // 2)) for n in range(nx)])
    got = lax.all_to_all(
        call(pair_kernel, (ny // 2, *piece), mine, theirs), "gy", 0, 0, axis_index_groups=cores
    )
    mine = call(sum_kernel, theirs.shape, got)
    theirs = lax.ppermute(mine, "gy", swap)
    factor_t, core = final_call(rank, mine, theirs, inv_scale, start, data)
    return (core, factor_t.T)


def solution(mesh):
    in_specs = (P(None, "gx", "gy"), P(), P(), P())
    out_specs = (P(None, "gx", "gy"), P())
    return jax.shard_map(body, mesh=mesh, in_specs=in_specs, out_specs=out_specs, check_vma=False)
```
